32 devices in a mesh: dp: 4 (over x, core), ctx: 8 (over z, y).
Axes of the slice: x: 2, y: 2, z: 4, core: 2. Of those that a mesh axis runs over, the one named last changes fastest.
Arguments:
- queries: bfloat16 [4096, 4096], P(('dp', 'ctx')), may hold values from -6 to 6
- key_proj: bfloat16 [4096, 512], P(('dp', 'ctx')), may hold values from -6 to 6
- value_proj: bfloat16 [4096, 512], P(('dp', 'ctx')), may hold values from -6 to 6
- out_grad: bfloat16 [4096, 4096], P(('dp', 'ctx')), may hold values from -6 to 6
- row_plan: int32 [4096], P(('dp', 'ctx')), may hold values from 0 to 127, as said below
- segments: int32 [4, 1024], P('dp', 'ctx'), may hold values from 0 to 5, as said below
Outputs:
- attended: bfloat16 [4096, 4096], P(('dp', 'ctx'))
- query_grad: bfloat16 [4096, 4096], P(('dp', 'ctx'))
- key_grad: bfloat16 [4096, 512], P(('dp', 'ctx'))
- value_grad: bfloat16 [4096, 512], P(('dp', 'ctx'))
The draws below stay inside these ranges and needn't reach their ends.
Inputs may be any that keep to these rules, and one draw needn't show every extreme that they name: `row_plan`: each aligned block of 128 entries (the rows of one device) is a permutation of 0 to 127. `segments`: along each row the ids never fall, and every id from 0 to 5 occurs. Every document has at most 640 positions, and in each row one document has exactly that many.
All inputs are finite; a program needn't handle non-finite values.
Results may differ from the reference program's by a relative error of at most 0.0083.
Values may be sent and summed in bfloat16 or wider, within the bound.
A program may use at most 128 MiB of HBM per device.

```python
import jax
import jax.numpy as jnp
from jax import lax

HEADS = 32
KV_HEADS = 4
HEAD_DIM = 128
TOK_DEV = 128
DOCS = 6
SPAN_DEV = 5
SEQ = 1024
TOKENS = 4096
N_DP = 4
N_CTX = 8


def plan_table(key):
    folded = jax.random.fold_in(key, 101)
    ranks = jax.random.randint(folded, (N_DP * N_CTX, TOK_DEV), 0, 1024, dtype=jnp.int32)
    ranks = ranks * TOK_DEV + jnp.arange(TOK_DEV, dtype=jnp.int32)[None, :]
    return jnp.argsort(ranks, axis=1).astype(jnp.int32)


def segment_table(key):
    folded = jax.random.fold_in(key, 202)
    streams = jax.random.split(folded, 2)
    longest = SPAN_DEV * TOK_DEV
    others = DOCS - 1
    rest = SEQ - longest
    even_len = rest // others
    base = even_len + (jnp.arange(others, dtype=jnp.int32) < rest % others).astype(jnp.int32)
    pairs = others // 2
    upper = max(min(even_len - 1, longest - even_len - 1), 1)
    lengths = jnp.broadcast_to(base[None, :], (N_DP, others)).astype(jnp.int32)
    if pairs > 0:
        moves = jax.random.randint(streams[0], (N_DP, pairs), 0, upper, dtype=jnp.int32)
        lengths = lengths.at[:, 0:2 * pairs:2].add(moves)
        lengths = lengths.at[:, 1:2 * pairs:2].add(-moves)
    lengths = jnp.concatenate([jnp.full((N_DP, 1), longest, jnp.int32), lengths], axis=1)
    turns = jax.random.randint(streams[1], (N_DP, 1), 0, DOCS, dtype=jnp.int32)
    order = (jnp.arange(DOCS, dtype=jnp.int32)[None, :] - turns) % DOCS
    lengths = jnp.take_along_axis(lengths, order, axis=1)
    cut_points = jnp.cumsum(lengths, axis=1)[:, :DOCS - 1].astype(jnp.int32)
    positions = jnp.arange(SEQ, dtype=jnp.int32)
    return jnp.sum((positions[None, :, None] >= cut_points[:, None, :]).astype(jnp.int32), axis=2).astype(jnp.int32)


def unpack_loader(packed, plan_rows):
    columns = packed.shape[2]
    share = TOK_DEV // N_DP
    slots = jnp.transpose(packed.reshape(N_DP, N_CTX, N_DP, share, columns), (2, 1, 0, 3, 4))
    slots = slots.reshape(N_DP * N_CTX * TOK_DEV, columns)
    starts = (jnp.arange(N_DP * N_CTX, dtype=jnp.int32) * TOK_DEV)[:, None]
    target = (starts + plan_rows).reshape(-1)
    return jnp.zeros_like(slots).at[target].set(slots)


def attention_pair(key):
    folded = jax.random.fold_in(key, 303)
    streams = jax.random.split(folded, 4)
    q_dims = (N_DP, SEQ, HEADS, HEAD_DIM)
    k_dims = (N_DP, SEQ, KV_HEADS, HEAD_DIM)
    q_vals = jax.random.normal(streams[1], q_dims)
    k_vals = jax.random.normal(streams[3], k_dims)
    q_vals = jnp.clip(q_vals, -6.0, 6.0).reshape(N_DP, SEQ, HEADS * HEAD_DIM)
    k_vals = jnp.clip(k_vals, -6.0, 6.0).reshape(N_DP, SEQ, KV_HEADS * HEAD_DIM)
    plan_rows = plan_table(key)
    return (unpack_loader(q_vals, plan_rows), unpack_loader(k_vals, plan_rows))


def draw_queries(key, part):
    return attention_pair(key)[0].astype(jnp.bfloat16)


def draw_key_proj(key, part):
    return attention_pair(key)[1].astype(jnp.bfloat16)


def draw_row_plan(key, part):
    return plan_table(key).reshape(-1)


def draw_segments(key, part):
    return segment_table(key)


def block_levels(own_key, dims, cuts, smallest, largest):
    loudness, own = 1.0, jax.random.fold_in(own_key, 6)
    for dim, parts in cuts:
        heights = jnp.exp(jax.random.uniform(jax.random.fold_in(own, dim), (parts,), jnp.float32, smallest / len(cuts), largest / len(cuts)))
        loudness = loudness * jnp.repeat(heights, dims[dim] // parts).reshape([-1 if axis == dim else 1 for axis in range(len(dims))])
    return loudness


def centred(stream_key, dims, scale, bound, cuts=(), kind=jnp.bfloat16):
    entries = scale * jax.random.normal(stream_key, dims, jnp.float32)
    if cuts:
        entries = entries * block_levels(stream_key, dims, cuts, -0.22, 0.18)
    return jnp.clip(entries, -bound, bound).astype(kind)


def setup_inputs(seed: int = 0) -> dict:
    streams_of = jax.random.split(jax.random.key(seed), 7)
    return {
        "queries": draw_queries(jax.random.fold_in(streams_of[6], 71), 0),
        "key_proj": draw_key_proj(jax.random.fold_in(streams_of[6], 71), 0),
        "value_proj": centred(streams_of[2], (TOKENS, KV_HEADS * HEAD_DIM), 1.0, 6.0, ((0, 32),)),
        "out_grad": centred(streams_of[3], (TOKENS, HEADS * HEAD_DIM), 1.0, 6.0, ((0, 32),)),
        "row_plan": draw_row_plan(jax.random.fold_in(streams_of[6], 71), 0),
        "segments": draw_segments(jax.random.fold_in(streams_of[6], 71), 0),
    }


NEG = -1.0e30


def slot_index(row_plan):
    starts = (jnp.arange(N_DP * N_CTX, dtype=jnp.int32) * TOK_DEV)[:, None]
    return (starts + row_plan.reshape(N_DP * N_CTX, TOK_DEV)).reshape(-1)


def pack_rows(loader_rows, row_plan):
    columns = loader_rows.shape[1]
    share = TOK_DEV // N_DP
    picked = loader_rows[slot_index(row_plan)]
    picked = picked.reshape(N_DP, N_CTX, N_DP, share, columns)
    return jnp.transpose(picked, (2, 1, 0, 3, 4)).reshape(N_DP, SEQ, columns)


def unpack_rows(packed, row_plan):
    columns = packed.shape[2]
    share = TOK_DEV // N_DP
    slots = jnp.transpose(packed.reshape(N_DP, N_CTX, N_DP, share, columns), (2, 1, 0, 3, 4))
    slots = slots.reshape(TOKENS, columns)
    return jnp.zeros_like(slots).at[slot_index(row_plan)].set(slots)


def group_attention(inputs):
    q_flat, k_flat, v_flat, d_flat, seg_all = inputs
    seq_len = q_flat.shape[0]
    groups = HEADS // KV_HEADS
    scaling = HEAD_DIM ** -0.5
    block_len = min(256, seq_len)
    blocks = seq_len // block_len
    keys_all = k_flat.reshape(seq_len, KV_HEADS, HEAD_DIM).astype(jnp.float32)
    vals_all = v_flat.reshape(seq_len, KV_HEADS, HEAD_DIM).astype(jnp.float32)
    positions = jnp.arange(seq_len, dtype=jnp.int32)

    def block_step(running, block_idx):
        k_total, v_total = running
        offset = (block_idx * block_len).astype(jnp.int32)
        q_heads = lax.dynamic_slice_in_dim(q_flat, offset, block_len, 0).reshape(block_len, KV_HEADS, groups, HEAD_DIM).astype(jnp.float32)
        d_heads = lax.dynamic_slice_in_dim(d_flat, offset, block_len, 0).reshape(block_len, KV_HEADS, groups, HEAD_DIM).astype(jnp.float32)
        seg_rows = lax.dynamic_slice_in_dim(seg_all, offset, block_len, 0)
        pos_rows = offset + jnp.arange(block_len, dtype=jnp.int32)
        raw_scores = jnp.einsum("qkgd,skd->kgqs", q_heads, keys_all) * scaling
        visible = (seg_all[None, :] == seg_rows[:, None]) & (positions[None, :] <= pos_rows[:, None])
        scores = jnp.where(visible, raw_scores, NEG)
        row_top = jnp.max(scores, axis=3)
        row_sum = jnp.sum(jnp.where(visible, jnp.exp(scores - row_top[..., None]), 0.0), axis=3)
        log_sum = row_top + jnp.log(row_sum)
        probs = jnp.where(visible, jnp.exp(scores - log_sum[..., None]), 0.0)
        weights = lax.optimization_barrier(probs.astype(jnp.bfloat16)).astype(jnp.float32)
        out = jnp.einsum("kgqs,skd->qkgd", weights, vals_all)
        row_dot = jnp.transpose(jnp.sum(d_heads * out, axis=3), (1, 2, 0))
        dprobs = jnp.einsum("qkgd,skd->kgqs", d_heads, vals_all)
        dscore = probs * (dprobs - row_dot[..., None]) * scaling
        dscore = lax.optimization_barrier(dscore.astype(jnp.bfloat16)).astype(jnp.float32)
        q_grad = jnp.einsum("kgqs,skd->qkgd", dscore, keys_all)
        k_total = k_total + jnp.einsum("kgqs,qkgd->skd", dscore, q_heads)
        v_total = v_total + jnp.einsum("kgqs,qkgd->skd", weights, d_heads)
        emitted = (out.astype(jnp.bfloat16).reshape(block_len, -1), q_grad.astype(jnp.bfloat16).reshape(block_len, -1))
        return (k_total, v_total), emitted

    zeros = jnp.zeros((seq_len, KV_HEADS, HEAD_DIM), jnp.float32)
    (k_total, v_total), (outs, q_grads) = lax.scan(block_step, (zeros, zeros), jnp.arange(blocks, dtype=jnp.int32))
    return (outs.reshape(seq_len, -1), q_grads.reshape(seq_len, -1),
            k_total.astype(jnp.bfloat16).reshape(seq_len, -1), v_total.astype(jnp.bfloat16).reshape(seq_len, -1))


def reference(queries, key_proj, value_proj, out_grad, row_plan, segments):
    packed = (pack_rows(queries, row_plan), pack_rows(key_proj, row_plan), pack_rows(value_proj, row_plan),
              pack_rows(out_grad, row_plan), segments)
    attended, q_grad, k_grad, v_grad = lax.map(group_attention, packed)
    return (unpack_rows(attended, row_plan), unpack_rows(q_grad, row_plan),
            unpack_rows(k_grad, row_plan), unpack_rows(v_grad, row_plan))
```

```python
import functools
import math

import jax
import jax.numpy as jnp
from jax import lax
from jax.experimental import pallas as pl
from jax.experimental.pallas import tpu as pltpu
from jax.sharding import PartitionSpec as P

HEADS = 32
KV_HEADS = 4
HEAD_DIM = 128
GROUP = HEADS // KV_HEADS
WIDE = GROUP * HEAD_DIM

NEG = -1e30
MESH = pl.DeviceIdType.MESH
F32 = jnp.float32
BF16 = jnp.bfloat16


def dot(lhs, rhs):
    return jnp.dot(lhs, rhs, preferred_element_type=F32)


def dot_nt(lhs, rhs):
    return lax.dot_general(lhs, rhs, (((1,), (1,)), ((), ())), preferred_element_type=F32)


def kernel(
    n_dp, n_ctx, reach,
    q_ref, k_ref, v_ref, d_ref, plan_ref, seg_ref,
    att_ref, qg_ref, kg_ref, vg_ref,
    kv_out, qd_out, kv, qd, segs, res, back, own, term_out, term_in, sum_out, sum_back,
    bias, q_cat, d_cat, w_t, ds_t,
    kv_s, kv_r, qd_s, qd_r, ctx_s, ctx_r, seg_s, seg_r, res_s, res_r, term_s, term_r, sum_s, sum_r,
):
    rows = q_ref.shape[0]
    share = rows // n_dp
    keys = (reach + 1) * rows
    scaling = HEAD_DIM ** (-0.5)
    a = lax.axis_index("dp")
    c = lax.axis_index("ctx")

    barrier = pltpu.get_barrier_semaphore()
    for i in range(1, n_dp):
        pl.semaphore_signal(
            barrier, inc=1, device_id={"dp": lax.rem(a + i, n_dp)}, device_id_type=MESH
        )
    for i in range(1, n_ctx):
        pl.semaphore_signal(
            barrier, inc=1, device_id={"ctx": lax.rem(c + i, n_ctx)}, device_id_type=MESH
        )

    def to_dp(src, dst, i, g, send, recv):
        peer = lax.rem(a + i, n_dp)
        return pltpu.make_async_remote_copy(
            src_ref=src.at[g, peer],
            dst_ref=dst(g),
            send_sem=send.at[g, i - 1],
            recv_sem=recv.at[g, i - 1],
            device_id={"dp": peer},
            device_id_type=MESH,
        )

    def kv_copy(g, i):
        return to_dp(kv_out, lambda g: kv.at[g, 0, a], i, g, kv_s, kv_r)

    def qd_copy(g, i):
        return to_dp(qd_out, lambda g: qd.at[g, a], i, g, qd_s, qd_r)

    def res_copy(g, i):
        return to_dp(res, lambda g: back.at[g, a], i, g, res_s, res_r)

    def sum_copy(g, i):
        return to_dp(sum_out, lambda g: sum_back.at[g, a], i, g, sum_s, sum_r)

    def ctx_copy(g, r):
        return pltpu.make_async_remote_copy(
            src_ref=kv.at[g, 0],
            dst_ref=kv.at[g, r],
            send_sem=ctx_s.at[g, r - 1],
            recv_sem=ctx_r.at[g, r - 1],
            device_id={"ctx": lax.rem(c + r, n_ctx)},
            device_id_type=MESH,
        )

    def seg_copy(r):
        return pltpu.make_async_remote_copy(
            src_ref=segs.at[0],
            dst_ref=segs.at[r],
            send_sem=seg_s.at[r - 1],
            recv_sem=seg_r.at[r - 1],
            device_id={"ctx": lax.rem(c + r, n_ctx)},
            device_id_type=MESH,
        )

    def term_copy(g, r):
        return pltpu.make_async_remote_copy(
            src_ref=term_out.at[g, r - 1],
            dst_ref=term_in.at[g, r - 1],
            send_sem=term_s.at[g, r - 1],
            recv_sem=term_r.at[g, r - 1],
            device_id={"ctx": lax.rem(c + n_ctx - r, n_ctx)},
            device_id_type=MESH,
        )

    heads = range(KV_HEADS)
    peers = range(1, n_dp)
    hops = range(1, reach + 1)

    def has_higher(r):
        return pl.when(c + r < n_ctx)

    def has_lower(r):
        return pl.when(c >= r)

    plan_row = jnp.broadcast_to(plan_ref[...], (rows, rows))
    unpack_f = jnp.where(
        lax.broadcasted_iota(jnp.int32, (rows, rows), 0) == plan_row, 1.0, 0.0
    ).astype(F32)
    unpack = unpack_f.astype(BF16)
    pack = unpack_f.T.astype(BF16)

    def packed(value):
        return dot(pack, value).astype(BF16).reshape(n_dp, share, value.shape[1])

    for g in heads:
        cols = slice(g * HEAD_DIM, (g + 1) * HEAD_DIM)
        kv_out[g, :, :, :HEAD_DIM] = packed(k_ref[:, cols])
        kv_out[g, :, :, HEAD_DIM:] = packed(v_ref[:, cols])
    segs[0] = jnp.broadcast_to(seg_ref[...], (8, rows))

    pl.semaphore_wait(barrier, n_dp - 1 + n_ctx - 1)

    for g in heads:
        for i in peers:
            kv_copy(g, i).start()
        kv[g, 0, a] = kv_out[g, a]
    for r in hops:

        @has_higher(r)
        def _():
            seg_copy(r).start()

    for g in heads:
        cols = slice(g * WIDE, (g + 1) * WIDE)
        qd_out[g, :, :, :WIDE] = packed(q_ref[:, cols])
        qd_out[g, :, :, WIDE:] = packed(d_ref[:, cols])
        for i in peers:
            qd_copy(g, i).start()
        qd[g, a] = qd_out[g, a]

    for g in heads:
        for i in peers:
            kv_copy(g, i).wait_recv()
        for r in hops:

            @has_higher(r)
            def _():
                ctx_copy(g, r).start()

    for r in hops:

        @pl.when(c < r)
        def _():
            segs[r] = jnp.full((8, rows), -1, jnp.int32)
            for g in heads:
                kv[g, r] = jnp.zeros(kv.shape[2:], BF16)

        @pl.when(c + r >= n_ctx)
        def _():
            for g in heads:
                term_in[g, r - 1] = jnp.zeros(term_in.shape[2:], BF16)

    for r in hops:

        @has_lower(r)
        def _():
            seg_copy(r).wait_recv()

    row_seg = jnp.broadcast_to(seg_ref[...], (rows, rows)).astype(F32)
    for r in range(reach + 1):
        key_seg = jnp.broadcast_to(segs[r, 0:1, :], (rows, rows)).astype(F32).T
        visible = key_seg == row_seg
        if r == 0:
            visible = visible & (
                lax.broadcasted_iota(jnp.int32, (rows, rows), 0)
                <= lax.broadcasted_iota(jnp.int32, (rows, rows), 1)
            )
        masked = jnp.where(visible, 0.0, NEG).astype(F32)
        bias[r * rows : (r + 1) * rows, :rows] = masked
        bias[r * rows : (r + 1) * rows, rows:] = masked

    def attend(g):
        k_blk = kv[g, :, :, :, :HEAD_DIM].reshape(keys, HEAD_DIM)
        v_blk = kv[g, :, :, :, HEAD_DIM:].reshape(keys, HEAD_DIM)
        for h in range(GROUP):
            into = slice(h * rows, (h + 1) * rows)
            cols = slice(h * HEAD_DIM, (h + 1) * HEAD_DIM)
            d_cols = slice(WIDE + h * HEAD_DIM, WIDE + (h + 1) * HEAD_DIM)
            q_cat[into, :] = qd[g, :, :, cols].reshape(rows, HEAD_DIM)
            d_cat[into, :] = qd[g, :, :, d_cols].reshape(rows, HEAD_DIM)

        def pair(step, carry):
            at = pl.multiple_of(step * (2 * rows), 2 * rows)
            span = pl.ds(at, 2 * rows)
            scores = dot_nt(k_blk, q_cat[span, :]) * (scaling * math.log2(math.e)) + bias[...]
            dprobs = dot_nt(v_blk, d_cat[span, :])
            top = jnp.max(scores, axis=0, keepdims=True)
            expd = jnp.exp2(scores - top)
            probs = expd * (1.0 / jnp.sum(expd, axis=0, keepdims=True))
            weights = probs.astype(BF16)
            w_t[:, span] = weights
            row_dot = jnp.sum(weights.astype(F32) * dprobs, axis=0, keepdims=True)
            ds_t[:, span] = (probs * (dprobs - row_dot) * scaling).astype(BF16)
            return carry

        lax.fori_loop(0, GROUP // 2, pair, 0)
        k_term = dot(ds_t[...], q_cat[...])
        v_term = dot(w_t[...], d_cat[...])
        own[g, :, :HEAD_DIM] = k_term[:rows]
        own[g, :, HEAD_DIM:] = v_term[:rows]
        for r in hops:
            part = slice(r * rows, (r + 1) * rows)
            term_out[g, r - 1, :, :HEAD_DIM] = k_term[part].astype(BF16)
            term_out[g, r - 1, :, HEAD_DIM:] = v_term[part].astype(BF16)
        for r in hops:

            @has_lower(r)
            def _():
                term_copy(g, r).start()

        v_t = v_blk.astype(F32).T.astype(BF16)
        k_t = k_blk.astype(F32).T.astype(BF16)
        out_t = dot(v_t, w_t[...])
        dq_t = dot(k_t, ds_t[...])
        for h in range(GROUP):
            part = slice(h * rows, (h + 1) * rows)
            cols = slice(h * HEAD_DIM, (h + 1) * HEAD_DIM)
            d_cols = slice(WIDE + h * HEAD_DIM, WIDE + (h + 1) * HEAD_DIM)
            res[g, :, :, cols] = out_t[:, part].T.astype(BF16).reshape(n_dp, share, HEAD_DIM)
            res[g, :, :, d_cols] = dq_t[:, part].T.astype(BF16).reshape(n_dp, share, HEAD_DIM)
        for i in peers:
            res_copy(g, i).start()
        back[g, a] = res[g, a]

    def finish_terms(g):
        total = own[g]
        for r in hops:

            @has_higher(r)
            def _():
                term_copy(g, r).wait_recv()

        for r in hops:
            total = total + term_in[g, r - 1].astype(F32)
        sum_out[g] = total.astype(BF16).reshape(n_dp, share, 2 * HEAD_DIM)
        for i in peers:
            sum_copy(g, i).start()
        sum_back[g, a] = sum_out[g, a]

    def finish_rows(g):
        for i in peers:
            res_copy(g, i).wait_recv()
        cols = slice(g * WIDE, (g + 1) * WIDE)
        got = back[g].reshape(rows, 2 * WIDE)
        att_ref[:, cols] = dot(unpack, got[:, :WIDE]).astype(BF16)
        qg_ref[:, cols] = dot(unpack, got[:, WIDE:]).astype(BF16)

    def finish_sums(g):
        for i in peers:
            sum_copy(g, i).wait_recv()
        cols = slice(g * HEAD_DIM, (g + 1) * HEAD_DIM)
        got = dot(unpack, sum_back[g].reshape(rows, 2 * HEAD_DIM)).astype(BF16)
        kg_ref[:, cols] = got[:, :HEAD_DIM]
        vg_ref[:, cols] = got[:, HEAD_DIM:]

    for g in heads:
        for i in peers:
            qd_copy(g, i).wait_recv()
        for r in hops:

            @has_lower(r)
            def _():
                ctx_copy(g, r).wait_recv()

        attend(g)
        if g >= 1:
            finish_terms(g - 1)
        if g >= 2:
            finish_rows(g - 2)
    last = KV_HEADS - 1
    finish_rows(last - 1)
    finish_terms(last)
    finish_rows(last)
    for g in heads:
        finish_sums(g)

    for g in heads:
        for i in peers:
            kv_copy(g, i).wait_send()
            qd_copy(g, i).wait_send()
            res_copy(g, i).wait_send()
            sum_copy(g, i).wait_send()
    for r in hops:

        @has_higher(r)
        def _():
            seg_copy(r).wait_send()
            for g in heads:
                ctx_copy(g, r).wait_send()

        @has_lower(r)
        def _():
            for g in heads:
                term_copy(g, r).wait_send()


def on_device(queries, key_proj, value_proj, out_grad, row_plan, segments):
    n_dp = lax.axis_size("dp")
    n_ctx = lax.axis_size("ctx")
    rows = queries.shape[0]
    share = rows // n_dp
    reach = min(n_ctx // 2 + 1, n_ctx - 1)
    keys = (reach + 1) * rows
    stacked = GROUP * rows
    vmem = pl.BlockSpec(memory_space=pltpu.VMEM)
    dma = pltpu.SemaphoreType.DMA
    dp_sem = dma((KV_HEADS, n_dp - 1))
    hop_sem = dma((KV_HEADS, reach))
    narrow = (n_dp, share, 2 * HEAD_DIM)
    broad = (KV_HEADS, n_dp, share, 2 * WIDE)
    scratch = [
        pltpu.VMEM((KV_HEADS, *narrow), BF16),
        pltpu.VMEM(broad, BF16),
        pltpu.VMEM((KV_HEADS, reach + 1, *narrow), BF16),
        pltpu.VMEM(broad, BF16),
        pltpu.VMEM((reach + 1, 8, rows), jnp.int32),
        pltpu.VMEM(broad, BF16),
        pltpu.VMEM(broad, BF16),
        pltpu.VMEM((KV_HEADS, rows, 2 * HEAD_DIM), F32),
        pltpu.VMEM((KV_HEADS, reach, rows, 2 * HEAD_DIM), BF16),
        pltpu.VMEM((KV_HEADS, reach, rows, 2 * HEAD_DIM), BF16),
        pltpu.VMEM((KV_HEADS, *narrow), BF16),
        pltpu.VMEM((KV_HEADS, *narrow), BF16),
        pltpu.VMEM((keys, 2 * rows), F32),
        pltpu.VMEM((stacked, HEAD_DIM), BF16),
        pltpu.VMEM((stacked, HEAD_DIM), BF16),
        pltpu.VMEM((keys, stacked), BF16),
        pltpu.VMEM((keys, stacked), BF16),
        dp_sem, dp_sem,
        dp_sem, dp_sem,
        hop_sem, hop_sem,
        dma((reach,)), dma((reach,)),
        dp_sem, dp_sem,
        hop_sem, hop_sem,
        dp_sem, dp_sem,
    ]
    return pl.pallas_call(
        functools.partial(kernel, n_dp, n_ctx, reach),
        out_shape=(
            jax.ShapeDtypeStruct(queries.shape, BF16),
            jax.ShapeDtypeStruct(queries.shape, BF16),
            jax.ShapeDtypeStruct(key_proj.shape, BF16),
            jax.ShapeDtypeStruct(value_proj.shape, BF16),
        ),
        in_specs=[vmem] * 6,
        out_specs=(vmem,) * 4,
        scratch_shapes=scratch,
        compiler_params=pltpu.CompilerParams(
            collective_id=0, has_side_effects=True, vmem_limit_bytes=56 * 1024 * 1024
        ),
        cost_estimate=pl.CostEstimate(
            flops=12 * HEADS * rows * keys * HEAD_DIM,
            bytes_accessed=4 * queries.size * 2,
            transcendentals=HEADS * rows * keys,
        ),
    )(queries, key_proj, value_proj, out_grad, row_plan.reshape(1, rows), segments)


def solution(mesh):
    placed = (
        P(("dp", "ctx"), None),
        P(("dp", "ctx"), None),
        P(("dp", "ctx"), None),
        P(("dp", "ctx"), None),
        P(("dp", "ctx")),
        P("dp", "ctx"),
    )
    return jax.shard_map(
        on_device,
        mesh=mesh,
        in_specs=placed,
        out_specs=(
            P(("dp", "ctx"), None),
            P(("dp", "ctx"), None),
            P(("dp", "ctx"), None),
            P(("dp", "ctx"), None),
        ),
        check_vma=False,
    )
```

```python
import functools
import math

import jax
import jax.numpy as jnp
from jax import lax
from jax.experimental import pallas as pl
from jax.experimental.pallas import tpu as pltpu
from jax.sharding import PartitionSpec as P

HEADS = 32
KV_HEADS = 4
HEAD_DIM = 128
GROUP = HEADS // KV_HEADS
WIDE = GROUP * HEAD_DIM

NEG = -1e30
MESH = pl.DeviceIdType.MESH
F32 = jnp.float32
BF16 = jnp.bfloat16


def dot(lhs, rhs):
    return jnp.dot(lhs, rhs, preferred_element_type=F32)


def dot_nt(lhs, rhs):
    return lax.dot_general(lhs, rhs, (((1,), (1,)), ((), ())), preferred_element_type=F32)


def unpacking(plan_ref):
    rows = plan_ref.shape[1]
    plan_row = jnp.broadcast_to(plan_ref[...], (rows, rows))
    here = lax.broadcasted_iota(jnp.int32, (rows, rows), 0) == plan_row
    return jnp.where(here, 1.0, 0.0).astype(F32)


def unpack_kernel(plan_ref, back_ref, sums_ref, att_ref, qg_ref, kg_ref, vg_ref):
    rows = plan_ref.shape[1]
    unpack = unpacking(plan_ref).astype(BF16)
    got = back_ref[0].reshape(rows, 2 * WIDE)
    att_ref[...] = dot(unpack, got[:, :WIDE]).astype(BF16)
    qg_ref[...] = dot(unpack, got[:, WIDE:]).astype(BF16)
    sums = dot(unpack, sums_ref[0].reshape(rows, 2 * HEAD_DIM)).astype(BF16)
    kg_ref[...] = sums[:, :HEAD_DIM]
    vg_ref[...] = sums[:, HEAD_DIM:]


def kernel(
    n_dp, n_ctx, reach,
    q_ref, k_ref, v_ref, d_ref, plan_ref, seg_ref,
    back, sum_back,
    kv_out, qd_out, kv, qd, segs, res, own, term_out, term_in, sum_out,
    bias, q_cat, d_cat, w_t, ds_t,
    kv_s, kv_r, qd_s, qd_r, ctx_s, ctx_r, beside_s, seg_s, seg_r, res_s, res_r, term_s, term_r, sum_s, sum_r,
):
    rows = q_ref.shape[0]
    share = rows // n_dp
    keys = (reach + 1) * rows
    scaling = HEAD_DIM ** (-0.5)
    a = lax.axis_index("dp")
    c = lax.axis_index("ctx")

    barrier = pltpu.get_barrier_semaphore()
    for i in range(1, n_dp):
        pl.semaphore_signal(
            barrier, inc=1, device_id={"dp": lax.rem(a + i, n_dp)}, device_id_type=MESH
        )
    for i in range(1, n_ctx):
        pl.semaphore_signal(
            barrier, inc=1, device_id={"ctx": lax.rem(c + i, n_ctx)}, device_id_type=MESH
        )

    def to_dp(src, dst, i, g, send, recv):
        peer = lax.rem(a + i, n_dp)
        return pltpu.make_async_remote_copy(
            src_ref=src.at[g, peer],
            dst_ref=dst(g),
            send_sem=send.at[g, i - 1],
            recv_sem=recv.at[g, i - 1],
            device_id={"dp": peer},
            device_id_type=MESH,
        )

    def kv_copy(g, i):
        return to_dp(kv_out, lambda g: kv.at[g, 0, a], i, g, kv_s, kv_r)

    def qd_copy(g, i):
        return to_dp(qd_out, lambda g: qd.at[g, a], i, g, qd_s, qd_r)

    def res_copy(g, i):
        return to_dp(res, lambda g: back.at[g, a], i, g, res_s, res_r)

    def sum_copy(g, i):
        return to_dp(sum_out, lambda g: sum_back.at[g, a], i, g, sum_s, sum_r)

    def ctx_copy(g, r):
        return pltpu.make_async_remote_copy(
            src_ref=kv.at[g, 0],
            dst_ref=kv.at[g, r],
            send_sem=ctx_s.at[g, r - 1],
            recv_sem=ctx_r.at[g, r - 1],
            device_id={"ctx": lax.rem(c + r, n_ctx)},
            device_id_type=MESH,
        )

    def beside_copy(g, r):
        low = lax.rem(c, 2) == 0
        there = jnp.where(low, r + 1, r - 1) if r else r + 1
        return pltpu.make_async_remote_copy(
            src_ref=kv.at[g, r],
            dst_ref=kv.at[g, there],
            send_sem=beside_s.at[g, r // 2],
            recv_sem=ctx_r.at[g, there - 1],
            device_id={"ctx": jnp.where(low, c + 1, c - 1)},
            device_id_type=MESH,
        )

    def beside(r):
        low = lax.rem(c, 2) == 0
        if r == 0:
            return pl.when(low)
        if r + 1 <= reach:
            return pl.when(c >= r)
        return pl.when((c >= r) & jnp.logical_not(low))

    def far(r):
        if r % 2 == 0:
            return pl.when(c + r < n_ctx)
        return pl.when((c + r < n_ctx) & (lax.rem(c, 2) == 1))

    straight = [r for r in range(1, reach + 1) if r % 2 == 0 or r == reach]
    passed = range(0, reach + 1, 2)

    def seg_copy(r):
        return pltpu.make_async_remote_copy(
            src_ref=segs.at[0],
            dst_ref=segs.at[r],
            send_sem=seg_s.at[r - 1],
            recv_sem=seg_r.at[r - 1],
            device_id={"ctx": lax.rem(c + r, n_ctx)},
            device_id_type=MESH,
        )

    def term_copy(g, r):
        return pltpu.make_async_remote_copy(
            src_ref=term_out.at[g, r - 1],
            dst_ref=term_in.at[g, r - 1],
            send_sem=term_s.at[g, r - 1],
            recv_sem=term_r.at[g, r - 1],
            device_id={"ctx": lax.rem(c + n_ctx - r, n_ctx)},
            device_id_type=MESH,
        )

    heads = range(KV_HEADS)
    peers = range(1, n_dp)
    hops = range(1, reach + 1)

    def has_higher(r):
        return pl.when(c + r < n_ctx)

    def has_lower(r):
        return pl.when(c >= r)

    pack = unpacking(plan_ref).T.astype(BF16)

    def packed(value):
        return dot(pack, value).astype(BF16).reshape(n_dp, share, value.shape[1])

    for g in heads:
        cols = slice(g * HEAD_DIM, (g + 1) * HEAD_DIM)
        kv_out[g, :, :, :HEAD_DIM] = packed(k_ref[:, cols])
        kv_out[g, :, :, HEAD_DIM:] = packed(v_ref[:, cols])
    segs[0] = jnp.broadcast_to(seg_ref[...], (8, rows))

    pl.semaphore_wait(barrier, n_dp - 1 + n_ctx - 1)

    for g in heads:
        for i in peers:
            kv_copy(g, i).start()
        kv[g, 0, a] = kv_out[g, a]
    for r in hops:

        @has_higher(r)
        def _():
            seg_copy(r).start()

    for g in heads:
        cols = slice(g * WIDE, (g + 1) * WIDE)
        qd_out[g, :, :, :WIDE] = packed(q_ref[:, cols])
        qd_out[g, :, :, WIDE:] = packed(d_ref[:, cols])
        for i in peers:
            qd_copy(g, i).start()
        qd[g, a] = qd_out[g, a]

    for g in heads:
        for i in peers:
            kv_copy(g, i).wait_recv()
        for r in straight:

            @far(r)
            def _():
                ctx_copy(g, r).start()

        @beside(0)
        def _():
            beside_copy(g, 0).start()

    for r in hops:

        @pl.when(c < r)
        def _():
            segs[r] = jnp.full((8, rows), -1, jnp.int32)
            for g in heads:
                kv[g, r] = jnp.zeros(kv.shape[2:], BF16)

        @pl.when(c + r >= n_ctx)
        def _():
            for g in heads:
                term_in[g, r - 1] = jnp.zeros(term_in.shape[2:], BF16)

    for r in hops:

        @has_lower(r)
        def _():
            seg_copy(r).wait_recv()

    row_seg = jnp.broadcast_to(seg_ref[...], (rows, rows)).astype(F32)
    for r in range(reach + 1):
        key_seg = jnp.broadcast_to(segs[r, 0:1, :], (rows, rows)).astype(F32).T
        visible = key_seg == row_seg
        if r == 0:
            visible = visible & (
                lax.broadcasted_iota(jnp.int32, (rows, rows), 0)
                <= lax.broadcasted_iota(jnp.int32, (rows, rows), 1)
            )
        masked = jnp.where(visible, 0.0, NEG).astype(F32)
        bias[r * rows : (r + 1) * rows, :rows] = masked
        bias[r * rows : (r + 1) * rows, rows:] = masked

    def attend(g):
        k_blk = kv[g, :, :, :, :HEAD_DIM].reshape(keys, HEAD_DIM)
        v_blk = kv[g, :, :, :, HEAD_DIM:].reshape(keys, HEAD_DIM)
        for h in range(GROUP):
            into = slice(h * rows, (h + 1) * rows)
            cols = slice(h * HEAD_DIM, (h + 1) * HEAD_DIM)
            d_cols = slice(WIDE + h * HEAD_DIM, WIDE + (h + 1) * HEAD_DIM)
            q_cat[into, :] = qd[g, :, :, cols].reshape(rows, HEAD_DIM)
            d_cat[into, :] = qd[g, :, :, d_cols].reshape(rows, HEAD_DIM)

        def pair(step, carry):
            at = pl.multiple_of(step * (2 * rows), 2 * rows)
            span = pl.ds(at, 2 * rows)
            scores = dot_nt(k_blk, q_cat[span, :]) * (scaling * math.log2(math.e)) + bias[...]
            dprobs = dot_nt(v_blk, d_cat[span, :])
            top = jnp.max(scores, axis=0, keepdims=True)
            expd = jnp.exp2(scores - top)
            probs = expd * (1.0 / jnp.sum(expd, axis=0, keepdims=True))
            weights = probs.astype(BF16)
            w_t[:, span] = weights
            row_dot = jnp.sum(weights.astype(F32) * dprobs, axis=0, keepdims=True)
            ds_t[:, span] = (probs * (dprobs - row_dot) * scaling).astype(BF16)
            return carry

        lax.fori_loop(0, GROUP // 2, pair, 0)
        k_term = dot(ds_t[...], q_cat[...])
        v_term = dot(w_t[...], d_cat[...])
        own[g, :, :HEAD_DIM] = k_term[:rows]
        own[g, :, HEAD_DIM:] = v_term[:rows]
        for r in hops:
            part = slice(r * rows, (r + 1) * rows)
            term_out[g, r - 1, :, :HEAD_DIM] = k_term[part].astype(BF16)
            term_out[g, r - 1, :, HEAD_DIM:] = v_term[part].astype(BF16)
        for r in hops:

            @has_lower(r)
            def _():
                term_copy(g, r).start()

        v_t = v_blk.astype(F32).T.astype(BF16)
        k_t = k_blk.astype(F32).T.astype(BF16)
        out_t = dot(v_t, w_t[...])
        dq_t = dot(k_t, ds_t[...])
        for h in range(GROUP):
            part = slice(h * rows, (h + 1) * rows)
            cols = slice(h * HEAD_DIM, (h + 1) * HEAD_DIM)
            d_cols = slice(WIDE + h * HEAD_DIM, WIDE + (h + 1) * HEAD_DIM)
            res[g, :, :, cols] = out_t[:, part].T.astype(BF16).reshape(n_dp, share, HEAD_DIM)
            res[g, :, :, d_cols] = dq_t[:, part].T.astype(BF16).reshape(n_dp, share, HEAD_DIM)
        for i in peers:
            res_copy(g, i).start()
        back[g, a] = res[g, a]

    def finish_terms(g):
        total = own[g]
        for r in hops:

            @has_higher(r)
            def _():
                term_copy(g, r).wait_recv()

        for r in hops:
            total = total + term_in[g, r - 1].astype(F32)
        sum_out[g] = total.astype(BF16).reshape(n_dp, share, 2 * HEAD_DIM)
        for i in peers:
            sum_copy(g, i).start()
        sum_back[g, a] = sum_out[g, a]

    def pass_on(g):
        for r in passed[1:]:

            @has_lower(r)
            def _():
                ctx_copy(g, r).wait_recv()

            @beside(r)
            def _():
                beside_copy(g, r).start()

    pass_on(0)
    for g in heads:
        if g + 1 < KV_HEADS:
            pass_on(g + 1)
        for i in peers:
            qd_copy(g, i).wait_recv()
        for r in hops[::2]:

            @has_lower(r)
            def _():
                ctx_copy(g, r).wait_recv()

        attend(g)
        if g >= 1:
            finish_terms(g - 1)
    finish_terms(KV_HEADS - 1)
    for g in heads:
        for i in peers:
            res_copy(g, i).wait_recv()
            sum_copy(g, i).wait_recv()

    for g in heads:
        for i in peers:
            kv_copy(g, i).wait_send()
            qd_copy(g, i).wait_send()
            res_copy(g, i).wait_send()
            sum_copy(g, i).wait_send()
    for r in hops:

        @has_higher(r)
        def _():
            seg_copy(r).wait_send()

        @has_lower(r)
        def _():
            for g in heads:
                term_copy(g, r).wait_send()

    for r in straight:

        @far(r)
        def _():
            for g in heads:
                ctx_copy(g, r).wait_send()

    for r in passed:

        @beside(r)
        def _():
            for g in heads:
                beside_copy(g, r).wait_send()


def on_device(queries, key_proj, value_proj, out_grad, row_plan, segments):
    n_dp = lax.axis_size("dp")
    n_ctx = lax.axis_size("ctx")
    rows = queries.shape[0]
    share = rows // n_dp
    reach = min(n_ctx // 2 + 1, n_ctx - 1)
    keys = (reach + 1) * rows
    stacked = GROUP * rows
    vmem = pl.BlockSpec(memory_space=pltpu.VMEM)
    dma = pltpu.SemaphoreType.DMA
    dp_sem = dma((KV_HEADS, n_dp - 1))
    hop_sem = dma((KV_HEADS, reach))
    narrow = (n_dp, share, 2 * HEAD_DIM)
    broad = (KV_HEADS, n_dp, share, 2 * WIDE)
    scratch = [
        pltpu.VMEM((KV_HEADS, *narrow), BF16),
        pltpu.VMEM(broad, BF16),
        pltpu.VMEM((KV_HEADS, reach + 1, *narrow), BF16),
        pltpu.VMEM(broad, BF16),
        pltpu.VMEM((reach + 1, 8, rows), jnp.int32),
        pltpu.VMEM(broad, BF16),
        pltpu.VMEM((KV_HEADS, rows, 2 * HEAD_DIM), F32),
        pltpu.VMEM((KV_HEADS, reach, rows, 2 * HEAD_DIM), BF16),
        pltpu.VMEM((KV_HEADS, reach, rows, 2 * HEAD_DIM), BF16),
        pltpu.VMEM((KV_HEADS, *narrow), BF16),
        pltpu.VMEM((keys, 2 * rows), F32),
        pltpu.VMEM((stacked, HEAD_DIM), BF16),
        pltpu.VMEM((stacked, HEAD_DIM), BF16),
        pltpu.VMEM((keys, stacked), BF16),
        pltpu.VMEM((keys, stacked), BF16),
        dp_sem, dp_sem,
        dp_sem, dp_sem,
        hop_sem, hop_sem,
        dma((KV_HEADS, reach // 2 + 1)),
        dma((reach,)), dma((reach,)),
        dp_sem, dp_sem,
        hop_sem, hop_sem,
        dp_sem, dp_sem,
    ]
    plan = row_plan.reshape(1, rows)
    back, sums = pl.pallas_call(
        functools.partial(kernel, n_dp, n_ctx, reach),
        out_shape=(
            jax.ShapeDtypeStruct(broad, BF16),
            jax.ShapeDtypeStruct((KV_HEADS, *narrow), BF16),
        ),
        in_specs=[vmem] * 6,
        out_specs=(vmem,) * 2,
        scratch_shapes=scratch,
        compiler_params=pltpu.CompilerParams(
            collective_id=0, has_side_effects=True, vmem_limit_bytes=56 * 1024 * 1024
        ),
        cost_estimate=pl.CostEstimate(
            flops=12 * HEADS * rows * keys * HEAD_DIM,
            bytes_accessed=4 * queries.size * 2,
            transcendentals=HEADS * rows * keys,
        ),
    )(queries, key_proj, value_proj, out_grad, plan, segments)
    wide_block = pl.BlockSpec((rows, WIDE), lambda g: (0, g))
    head_block = pl.BlockSpec((rows, HEAD_DIM), lambda g: (0, g))
    return pl.pallas_call(
        unpack_kernel,
        grid=(KV_HEADS,),
        out_shape=(
            jax.ShapeDtypeStruct(queries.shape, BF16),
            jax.ShapeDtypeStruct(queries.shape, BF16),
            jax.ShapeDtypeStruct(key_proj.shape, BF16),
            jax.ShapeDtypeStruct(value_proj.shape, BF16),
        ),
        in_specs=[
            pl.BlockSpec((1, rows), lambda g: (0, 0)),
            pl.BlockSpec((1, *broad[1:]), lambda g: (g, 0, 0, 0)),
            pl.BlockSpec((1, *narrow), lambda g: (g, 0, 0, 0)),
        ],
        out_specs=(wide_block, wide_block, head_block, head_block),
    )(plan, back, sums)


def solution(mesh):
    placed = (
        P(("dp", "ctx"), None),
        P(("dp", "ctx"), None),
        P(("dp", "ctx"), None),
        P(("dp", "ctx"), None),
        P(("dp", "ctx")),
        P("dp", "ctx"),
    )
    return jax.shard_map(
        on_device,
        mesh=mesh,
        in_specs=placed,
        out_specs=(
            P(("dp", "ctx"), None),
            P(("dp", "ctx"), None),
            P(("dp", "ctx"), None),
            P(("dp", "ctx"), None),
        ),
        check_vma=False,
    )
```

```python
import functools
import math

import jax
import jax.numpy as jnp
from jax import lax
from jax.experimental import pallas as pl
from jax.experimental.pallas import tpu as pltpu
from jax.sharding import PartitionSpec as P

HEADS = 32
KV_HEADS = 4
HEAD_DIM = 128
GROUP = HEADS // KV_HEADS
WIDE = GROUP * HEAD_DIM

NEG = -1e30
MESH = pl.DeviceIdType.MESH
F32 = jnp.float32
BF16 = jnp.bfloat16


def dot(lhs, rhs):
    return jnp.dot(lhs, rhs, preferred_element_type=F32)


def dot_nt(lhs, rhs):
    return lax.dot_general(lhs, rhs, (((1,), (1,)), ((), ())), preferred_element_type=F32)


def unpacking(plan_ref):
    rows = plan_ref.shape[1]
    plan_row = jnp.broadcast_to(plan_ref[...], (rows, rows))
    here = lax.broadcasted_iota(jnp.int32, (rows, rows), 0) == plan_row
    return jnp.where(here, 1.0, 0.0).astype(F32)


def unpack_kernel(plan_ref, back_ref, sums_ref, att_ref, qg_ref, kg_ref, vg_ref):
    rows = plan_ref.shape[1]
    unpack = unpacking(plan_ref).astype(BF16)
    got = back_ref[0].reshape(rows, 2 * WIDE)
    att_ref[...] = dot(unpack, got[:, :WIDE]).astype(BF16)
    qg_ref[...] = dot(unpack, got[:, WIDE:]).astype(BF16)
    sums = dot(unpack, sums_ref[0].reshape(rows, 2 * HEAD_DIM)).astype(BF16)
    kg_ref[...] = sums[:, :HEAD_DIM]
    vg_ref[...] = sums[:, HEAD_DIM:]


def kernel(
    n_dp, n_ctx, reach,
    q_ref, k_ref, v_ref, d_ref, plan_ref, seg_ref,
    back, sum_back,
    q_in, d_in, kv_out, qd_out, kv, qd, segs, res, own, term_out, term_in, sum_out,
    bias, q_cat, d_cat, w_t, ds_t,
    fetch_sem, kv_s, kv_r, qd_s, qd_r, ctx_s, ctx_r, beside_s, seg_s, seg_r, res_s, res_r, term_s, term_r, sum_s, sum_r,
):
    rows = q_ref.shape[0]
    share = rows // n_dp
    keys = (reach + 1) * rows
    scaling = HEAD_DIM ** (-0.5)
    a = lax.axis_index("dp")
    c = lax.axis_index("ctx")

    fetches = (
        pltpu.make_async_copy(q_ref, q_in, fetch_sem.at[0]),
        pltpu.make_async_copy(d_ref, d_in, fetch_sem.at[1]),
    )
    for fetch in fetches:
        fetch.start()
    barrier = pltpu.get_barrier_semaphore()
    for i in range(1, n_dp):
        pl.semaphore_signal(
            barrier, inc=1, device_id={"dp": lax.rem(a + i, n_dp)}, device_id_type=MESH
        )
    for i in range(1, n_ctx):
        pl.semaphore_signal(
            barrier, inc=1, device_id={"ctx": lax.rem(c + i, n_ctx)}, device_id_type=MESH
        )

    def to_dp(src, dst, i, g, send, recv):
        peer = lax.rem(a + 2 * (i // 2), n_dp)
        if i % 2:
            peer = peer + 1 - 2 * lax.rem(peer, 2)
        return pltpu.make_async_remote_copy(
            src_ref=src.at[g, peer],
            dst_ref=dst(g),
            send_sem=send.at[g, i - 1],
            recv_sem=recv.at[g, i - 1],
            device_id={"dp": peer},
            device_id_type=MESH,
        )

    def kv_copy(g, i):
        return to_dp(kv_out, lambda g: kv.at[g, 0, a], i, g, kv_s, kv_r)

    def qd_copy(g, i):
        return to_dp(qd_out, lambda g: qd.at[g, a], i, g, qd_s, qd_r)

    def res_copy(g, i):
        return to_dp(res, lambda g: back.at[g, a], i, g, res_s, res_r)

    def sum_copy(g, i):
        return to_dp(sum_out, lambda g: sum_back.at[g, a], i, g, sum_s, sum_r)

    def ctx_copy(g, r):
        return pltpu.make_async_remote_copy(
            src_ref=kv.at[g, 0],
            dst_ref=kv.at[g, r],
            send_sem=ctx_s.at[g, r - 1],
            recv_sem=ctx_r.at[g, r - 1],
            device_id={"ctx": lax.rem(c + r, n_ctx)},
            device_id_type=MESH,
        )

    def beside_copy(g, r):
        low = lax.rem(c, 2) == 0
        there = jnp.where(low, r + 1, r - 1) if r else r + 1
        return pltpu.make_async_remote_copy(
            src_ref=kv.at[g, r],
            dst_ref=kv.at[g, there],
            send_sem=beside_s.at[g, r // 2],
            recv_sem=ctx_r.at[g, there - 1],
            device_id={"ctx": jnp.where(low, c + 1, c - 1)},
            device_id_type=MESH,
        )

    def beside(r):
        low = lax.rem(c, 2) == 0
        if r == 0:
            return pl.when(low)
        if r + 1 <= reach:
            return pl.when(c >= r)
        return pl.when((c >= r) & jnp.logical_not(low))

    def far(r):
        if r % 2 == 0:
            return pl.when(c + r < n_ctx)
        return pl.when((c + r < n_ctx) & (lax.rem(c, 2) == 1))

    straight = [r for r in range(1, reach + 1) if r % 2 == 0 or r == reach]
    passed = range(0, reach + 1, 2)

    def seg_copy(r):
        return pltpu.make_async_remote_copy(
            src_ref=segs.at[0],
            dst_ref=segs.at[r],
            send_sem=seg_s.at[r - 1],
            recv_sem=seg_r.at[r - 1],
            device_id={"ctx": lax.rem(c + r, n_ctx)},
            device_id_type=MESH,
        )

    def term_copy(g, r):
        return pltpu.make_async_remote_copy(
            src_ref=term_out.at[g, r - 1],
            dst_ref=term_in.at[g, r - 1],
            send_sem=term_s.at[g, r - 1],
            recv_sem=term_r.at[g, r - 1],
            device_id={"ctx": lax.rem(c + n_ctx - r, n_ctx)},
            device_id_type=MESH,
        )

    heads = range(KV_HEADS)
    peers = [*range(2, n_dp), 1]
    hops = range(1, reach + 1)

    def has_higher(r):
        return pl.when(c + r < n_ctx)

    def has_lower(r):
        return pl.when(c >= r)

    pack = unpacking(plan_ref).T.astype(BF16)

    def packed(value):
        return dot(pack, value).astype(BF16).reshape(n_dp, share, value.shape[1])

    for g in heads:
        cols = slice(g * HEAD_DIM, (g + 1) * HEAD_DIM)
        kv_out[g, :, :, :HEAD_DIM] = packed(k_ref[:, cols])
        kv_out[g, :, :, HEAD_DIM:] = packed(v_ref[:, cols])
    segs[0] = jnp.broadcast_to(seg_ref[...], (8, rows))

    pl.semaphore_wait(barrier, n_dp - 1 + n_ctx - 1)

    for g in heads:
        for i in peers:
            kv_copy(g, i).start()
        kv[g, 0, a] = kv_out[g, a]
    for r in hops:

        @has_higher(r)
        def _():
            seg_copy(r).start()

    for fetch in fetches:
        fetch.wait()
    for g in heads:
        cols = slice(g * WIDE, (g + 1) * WIDE)
        qd_out[g, :, :, :WIDE] = packed(q_in[:, cols])
        qd_out[g, :, :, WIDE:] = packed(d_in[:, cols])
        for i in peers:
            qd_copy(g, i).start()
        qd[g, a] = qd_out[g, a]

    for g in heads:
        for i in peers:
            kv_copy(g, i).wait_recv()
        for r in straight:

            @far(r)
            def _():
                ctx_copy(g, r).start()

        @beside(0)
        def _():
            beside_copy(g, 0).start()

    for r in hops:

        @pl.when(c < r)
        def _():
            segs[r] = jnp.full((8, rows), -1, jnp.int32)
            for g in heads:
                kv[g, r] = jnp.zeros(kv.shape[2:], BF16)

        @pl.when(c + r >= n_ctx)
        def _():
            for g in heads:
                term_in[g, r - 1] = jnp.zeros(term_in.shape[2:], BF16)

    for r in hops:

        @has_lower(r)
        def _():
            seg_copy(r).wait_recv()

    row_seg = jnp.broadcast_to(seg_ref[...], (rows, rows)).astype(F32)
    for r in range(reach + 1):
        key_seg = jnp.broadcast_to(segs[r, 0:1, :], (rows, rows)).astype(F32).T
        visible = key_seg == row_seg
        if r == 0:
            visible = visible & (
                lax.broadcasted_iota(jnp.int32, (rows, rows), 0)
                <= lax.broadcasted_iota(jnp.int32, (rows, rows), 1)
            )
        masked = jnp.where(visible, 0.0, NEG).astype(F32)
        bias[r * rows : (r + 1) * rows, :rows] = masked
        bias[r * rows : (r + 1) * rows, rows:] = masked

    def attend(g):
        k_blk = kv[g, :, :, :, :HEAD_DIM].reshape(keys, HEAD_DIM)
        v_blk = kv[g, :, :, :, HEAD_DIM:].reshape(keys, HEAD_DIM)
        for h in range(GROUP):
            into = slice(h * rows, (h + 1) * rows)
            cols = slice(h * HEAD_DIM, (h + 1) * HEAD_DIM)
            d_cols = slice(WIDE + h * HEAD_DIM, WIDE + (h + 1) * HEAD_DIM)
            q_cat[into, :] = qd[g, :, :, cols].reshape(rows, HEAD_DIM)
            d_cat[into, :] = qd[g, :, :, d_cols].reshape(rows, HEAD_DIM)

        def pair(step, carry):
            at = pl.multiple_of(step * (2 * rows), 2 * rows)
            span = pl.ds(at, 2 * rows)
            scores = dot_nt(k_blk, q_cat[span, :]) * (scaling * math.log2(math.e)) + bias[...]
            dprobs = dot_nt(v_blk, d_cat[span, :])
            top = jnp.max(scores, axis=0, keepdims=True)
            expd = jnp.exp2(scores - top)
            probs = expd * (1.0 / jnp.sum(expd, axis=0, keepdims=True))
            weights = probs.astype(BF16)
            w_t[:, span] = weights
            row_dot = jnp.sum(weights.astype(F32) * dprobs, axis=0, keepdims=True)
            ds_t[:, span] = (probs * (dprobs - row_dot) * scaling).astype(BF16)
            return carry

        lax.fori_loop(0, GROUP // 2, pair, 0)
        k_term = dot(ds_t[...], q_cat[...])
        v_term = dot(w_t[...], d_cat[...])
        own[g, :, :HEAD_DIM] = k_term[:rows]
        own[g, :, HEAD_DIM:] = v_term[:rows]
        for r in hops:
            part = slice(r * rows, (r + 1) * rows)
            term_out[g, r - 1, :, :HEAD_DIM] = k_term[part].astype(BF16)
            term_out[g, r - 1, :, HEAD_DIM:] = v_term[part].astype(BF16)
        for r in hops:

            @has_lower(r)
            def _():
                term_copy(g, r).start()

        v_t = v_blk.astype(F32).T.astype(BF16)
        k_t = k_blk.astype(F32).T.astype(BF16)
        out_t = dot(v_t, w_t[...])
        dq_t = dot(k_t, ds_t[...])
        for h in range(GROUP):
            part = slice(h * rows, (h + 1) * rows)
            cols = slice(h * HEAD_DIM, (h + 1) * HEAD_DIM)
            d_cols = slice(WIDE + h * HEAD_DIM, WIDE + (h + 1) * HEAD_DIM)
            res[g, :, :, cols] = out_t[:, part].T.astype(BF16).reshape(n_dp, share, HEAD_DIM)
            res[g, :, :, d_cols] = dq_t[:, part].T.astype(BF16).reshape(n_dp, share, HEAD_DIM)
        for i in peers:
            res_copy(g, i).start()
        back[g, a] = res[g, a]

    def finish_terms(g):
        total = own[g]
        for r in hops:

            @has_higher(r)
            def _():
                term_copy(g, r).wait_recv()

        for r in hops:
            total = total + term_in[g, r - 1].astype(F32)
        sum_out[g] = total.astype(BF16).reshape(n_dp, share, 2 * HEAD_DIM)
        for i in peers:
            sum_copy(g, i).start()
        sum_back[g, a] = sum_out[g, a]

    def pass_on(g):
        for r in passed[1:]:

            @has_lower(r)
            def _():
                ctx_copy(g, r).wait_recv()

            @beside(r)
            def _():
                beside_copy(g, r).start()

    pass_on(0)
    for g in heads:
        if g + 1 < KV_HEADS:
            pass_on(g + 1)
        for i in peers:
            qd_copy(g, i).wait_recv()
        for r in hops[::2]:

            @has_lower(r)
            def _():
                ctx_copy(g, r).wait_recv()

        attend(g)
        if g >= 1:
            finish_terms(g - 1)
    finish_terms(KV_HEADS - 1)
    for g in heads:
        for i in peers:
            res_copy(g, i).wait_recv()
            sum_copy(g, i).wait_recv()

    for g in heads:
        for i in peers:
            kv_copy(g, i).wait_send()
            qd_copy(g, i).wait_send()
            res_copy(g, i).wait_send()
            sum_copy(g, i).wait_send()
    for r in hops:

        @has_higher(r)
        def _():
            seg_copy(r).wait_send()

        @has_lower(r)
        def _():
            for g in heads:
                term_copy(g, r).wait_send()

    for r in straight:

        @far(r)
        def _():
            for g in heads:
                ctx_copy(g, r).wait_send()

    for r in passed:

        @beside(r)
        def _():
            for g in heads:
                beside_copy(g, r).wait_send()


def on_device(queries, key_proj, value_proj, out_grad, row_plan, segments):
    n_dp = lax.axis_size("dp")
    n_ctx = lax.axis_size("ctx")
    rows = queries.shape[0]
    share = rows // n_dp
    reach = min(n_ctx // 2 + 1, n_ctx - 1)
    keys = (reach + 1) * rows
    stacked = GROUP * rows
    vmem = pl.BlockSpec(memory_space=pltpu.VMEM)
    whole = pl.BlockSpec(memory_space=pl.ANY)
    dma = pltpu.SemaphoreType.DMA
    dp_sem = dma((KV_HEADS, n_dp - 1))
    hop_sem = dma((KV_HEADS, reach))
    narrow = (n_dp, share, 2 * HEAD_DIM)
    broad = (KV_HEADS, n_dp, share, 2 * WIDE)
    scratch = [
        pltpu.VMEM(queries.shape, BF16),
        pltpu.VMEM(queries.shape, BF16),
        pltpu.VMEM((KV_HEADS, *narrow), BF16),
        pltpu.VMEM(broad, BF16),
        pltpu.VMEM((KV_HEADS, reach + 1, *narrow), BF16),
        pltpu.VMEM(broad, BF16),
        pltpu.VMEM((reach + 1, 8, rows), jnp.int32),
        pltpu.VMEM(broad, BF16),
        pltpu.VMEM((KV_HEADS, rows, 2 * HEAD_DIM), F32),
        pltpu.VMEM((KV_HEADS, reach, rows, 2 * HEAD_DIM), BF16),
        pltpu.VMEM((KV_HEADS, reach, rows, 2 * HEAD_DIM), BF16),
        pltpu.VMEM((KV_HEADS, *narrow), BF16),
        pltpu.VMEM((keys, 2 * rows), F32),
        pltpu.VMEM((stacked, HEAD_DIM), BF16),
        pltpu.VMEM((stacked, HEAD_DIM), BF16),
        pltpu.VMEM((keys, stacked), BF16),
        pltpu.VMEM((keys, stacked), BF16),
        dma((2,)),
        dp_sem, dp_sem,
        dp_sem, dp_sem,
        hop_sem, hop_sem,
        dma((KV_HEADS, reach // 2 + 1)),
        dma((reach,)), dma((reach,)),
        dp_sem, dp_sem,
        hop_sem, hop_sem,
        dp_sem, dp_sem,
    ]
    plan = row_plan.reshape(1, rows)
    back, sums = pl.pallas_call(
        functools.partial(kernel, n_dp, n_ctx, reach),
        out_shape=(
            jax.ShapeDtypeStruct(broad, BF16),
            jax.ShapeDtypeStruct((KV_HEADS, *narrow), BF16),
        ),
        in_specs=[whole, vmem, vmem, whole, vmem, vmem],
        out_specs=(vmem,) * 2,
        scratch_shapes=scratch,
        compiler_params=pltpu.CompilerParams(
            collective_id=0, has_side_effects=True, vmem_limit_bytes=56 * 1024 * 1024
        ),
        cost_estimate=pl.CostEstimate(
            flops=12 * HEADS * rows * keys * HEAD_DIM,
            bytes_accessed=4 * queries.size * 2,
            transcendentals=HEADS * rows * keys,
        ),
    )(queries, key_proj, value_proj, out_grad, plan, segments)
    wide_block = pl.BlockSpec((rows, WIDE), lambda g: (0, g))
    head_block = pl.BlockSpec((rows, HEAD_DIM), lambda g: (0, g))
    return pl.pallas_call(
        unpack_kernel,
        grid=(KV_HEADS,),
        out_shape=(
            jax.ShapeDtypeStruct(queries.shape, BF16),
            jax.ShapeDtypeStruct(queries.shape, BF16),
            jax.ShapeDtypeStruct(key_proj.shape, BF16),
            jax.ShapeDtypeStruct(value_proj.shape, BF16),
        ),
        in_specs=[
            pl.BlockSpec((1, rows), lambda g: (0, 0)),
            pl.BlockSpec((1, *broad[1:]), lambda g: (g, 0, 0, 0)),
            pl.BlockSpec((1, *narrow), lambda g: (g, 0, 0, 0)),
        ],
        out_specs=(wide_block, wide_block, head_block, head_block),
    )(plan, back, sums)


def solution(mesh):
    placed = (
        P(("dp", "ctx"), None),
        P(("dp", "ctx"), None),
        P(("dp", "ctx"), None),
        P(("dp", "ctx"), None),
        P(("dp", "ctx")),
        P("dp", "ctx"),
    )
    return jax.shard_map(
        on_device,
        mesh=mesh,
        in_specs=placed,
        out_specs=(
            P(("dp", "ctx"), None),
            P(("dp", "ctx"), None),
            P(("dp", "ctx"), None),
            P(("dp", "ctx"), None),
        ),
        check_vma=False,
    )
```
